32 devices in a mesh: dp: 8 (over z, core), cp: 4 (over y, x).
Axes of the slice: x: 2, y: 2, z: 4, core: 2. Of those that a mesh axis runs over, the one named last changes fastest.
Arguments:
- queries: bfloat16 [4096, 3072], P(('dp', 'cp')), may hold values from -48 to 48
- key_heads: bfloat16 [4096, 512], P(('dp', 'cp')), may hold values from -6 to 6
- value_heads: bfloat16 [4096, 512], P(('dp', 'cp')), may hold values from -6 to 6
- segment_ids: int32 [8, 512], P('dp', 'cp'), may hold values from 0 to 1, never falling along the last dimension, each value on 1 to 384 neighbouring positions
- out_weight: bfloat16 [3072, 3072], P('dp', 'cp'), may hold values from -0.109375 to 0.109375
- grad_out: bfloat16 [4096, 3072], P('dp', 'cp'), may hold values from -6 to 6
Outputs:
- output: bfloat16 [4096, 3072], P('dp', 'cp')
- grad_queries: bfloat16 [4096, 3072], P(('dp', 'cp'))
- grad_keys: bfloat16 [4096, 512], P(('dp', 'cp'))
- grad_values: bfloat16 [4096, 512], P(('dp', 'cp'))
- grad_weight: float32 [3072, 3072], P('dp', 'cp')
The draws below stay inside these ranges and needn't reach their ends.
Inputs may be any that keep to these rules, and one draw needn't show every extreme that they name: `segment_ids`: document numbers of a group never fall; a document holds at most 384 positions.
All inputs are finite; a program needn't handle non-finite values.
Results may differ from the reference program's by a relative error of at most 0.023.
Values may be sent and summed in bfloat16 or wider, within the bound.
A program may use at most 128 MiB of HBM per device.

```python
import math
import jax
import jax.numpy as jnp
import numpy as np
from jax import lax

HQ = 24
HK = 4
HD = 128
DOUT = 3072
SEGS = 2
QW = 3072
KW = 512
GROUP = 512
TOKENS = 4096
N_DP = 8


def paired_keys(key):
    base_key = jax.random.fold_in(key, 101)
    drawn = jax.random.normal(base_key, (TOKENS, KW), jnp.float32)
    return jnp.clip(drawn, -6.0, 6.0)


def draw_key_heads(key, part):
    result = paired_keys(key)
    return result.astype(jnp.bfloat16)


def draw_queries(key, part):
    key = jax.random.fold_in(key, 5)
    result = jax.random.normal(key, (TOKENS, QW), jnp.float32)
    return jnp.clip(result, -48.0, 48.0).astype(jnp.bfloat16)


def block_levels(key, shape, cuts, smallest, top_value):
    factor_of = 1.0
    for dim, parts in cuts:
        draws = jax.random.uniform(jax.random.fold_in(jax.random.fold_in(key, 6), dim), (parts,), jnp.float32, smallest / len(cuts), top_value / len(cuts))
        factor_of = factor_of * jnp.repeat(jnp.exp(draws), shape[dim] // parts).reshape((-1,) + (1,) * (len(shape) - 1 - dim))
    return factor_of


def profile(number_of, total, bound, slope):
    weights = [(1 << 20) // math.isqrt(grade ** slope) + 1 for grade in range(2, number_of + 1)]
    rest, given = total - bound - (number_of - 1), [1] * (number_of - 1)
    while rest > 0:
        free = [i for i in range(number_of - 1) if given[i] < bound]
        whole, remaining = sum([weights[i] for i in free]), rest
        for i in free:
            extra = min(bound - given[i], max(1, remaining * weights[i] // whole), rest)
            given[i] = given[i] + extra
            rest = rest - extra
    return np.array([bound] + given)


def ragged_sizes(key, number_of, total, bound, slope):
    if number_of == 2:
        one = jax.random.randint(key, (), max(1, total - bound), min(bound, total - 1) + 1)
        return jnp.stack([one, total - one])
    tallies = jnp.asarray(profile(number_of, total, bound, slope), jnp.int32)
    pairs = (number_of - 1) // 2
    donor, receiver = tallies[1:1 + 2 * pairs:2], tallies[2:2 + 2 * pairs:2]
    room = jnp.minimum(donor - 1, bound - receiver)
    moved = jax.random.randint(jax.random.fold_in(key, 1), (pairs,), 0, 1 << 20) % (room + 1)
    tallies = tallies.at[1:1 + 2 * pairs:2].set(donor - moved).at[2:2 + 2 * pairs:2].set(receiver + moved)
    return tallies[jax.random.permutation(jax.random.fold_in(key, 2), number_of)]


def scatter_about(key, dims, width, reach, split=(), held_as=jnp.bfloat16):
    loudness = block_levels(key, dims, split, -0.22, 0.18) if split else 1.0
    values = jax.random.normal(key, dims, jnp.float32) * width * loudness
    return jnp.minimum(jnp.maximum(values, -reach), reach).astype(held_as)


def setup_inputs(seed: int = 0) -> dict:
    seeds = jax.random.split(jax.random.key(seed), 7)
    queries = draw_queries(jax.random.fold_in(seeds[6], 71), 0)
    key_heads = draw_key_heads(jax.random.fold_in(seeds[6], 71), 0)
    value_heads = scatter_about(seeds[2], (TOKENS, KW), 1.0, 6.0, ((0, 32),))
    segment_ids = jax.vmap(lambda own: jnp.searchsorted(jnp.cumsum(ragged_sizes(own, SEGS, GROUP, GROUP * 3 // 4, 2)), jnp.arange(GROUP), side="right"))(jax.random.split(seeds[3], N_DP)).reshape((N_DP, GROUP)).astype(jnp.int32)
    out_weight = scatter_about(seeds[4], (QW, DOUT), QW ** -0.5, 0.109375, ((0, 8), (1, 4)))
    grad_out = scatter_about(seeds[5], (TOKENS, DOUT), 1.0, 6.0, ((0, 8), (1, 4)))
    return {"queries": queries, "key_heads": key_heads, "value_heads": value_heads, "segment_ids": segment_ids, "out_weight": out_weight, "grad_out": grad_out}


def to_bf16(values_f32):
    return lax.optimization_barrier(values_f32.astype(jnp.bfloat16)).astype(jnp.float32)

def attend_group(group_queries, group_keys, group_values, group_segments, group_grad, weight):
    rows = group_queries.shape[0]
    head_share = HQ // HK
    score_scale = 1.0 / math.sqrt(HD)
    query_tiles = group_queries.astype(jnp.float32).reshape(rows, HK, head_share, HD)
    key_tiles = group_keys.astype(jnp.float32).reshape(rows, HK, HD)
    value_tiles = group_values.astype(jnp.float32).reshape(rows, HK, HD)
    logits = jnp.einsum('qhrd,khd->hrqk', query_tiles, key_tiles) * score_scale
    position = jnp.arange(rows, dtype=jnp.int32)
    allowed = (group_segments[:, None] == group_segments[None, :]) & (position[None, :] <= position[:, None])
    masked = jnp.where(allowed, logits, -1e+30)
    row_peak = lax.optimization_barrier(jnp.max(masked, axis=-1, keepdims=True))
    weights = jnp.where(allowed, jnp.exp(masked - row_peak), 0.0)
    probability = weights / lax.optimization_barrier(jnp.sum(weights, axis=-1, keepdims=True))
    rounded_prob = to_bf16(probability)
    attended = jnp.einsum('hrqk,khd->qhrd', rounded_prob, value_tiles).astype(jnp.bfloat16).reshape(rows, QW)
    output = jnp.dot(attended, weight, preferred_element_type=jnp.float32).astype(jnp.bfloat16)
    grad_attended = lax.dot_general(group_grad, weight, (((1,), (1,)), ((), ())), preferred_element_type=jnp.float32).astype(jnp.bfloat16)
    weight_partial = lax.dot_general(attended, group_grad, (((0,), (0,)), ((), ())), preferred_element_type=jnp.float32)
    grad_tiles = grad_attended.astype(jnp.float32).reshape(rows, HK, head_share, HD)
    grad_prob = jnp.einsum('qhrd,khd->hrqk', grad_tiles, value_tiles)
    delta = lax.optimization_barrier(jnp.sum(probability * grad_prob, axis=-1, keepdims=True))
    grad_logit = to_bf16(probability * (grad_prob - delta))
    grad_queries = (jnp.einsum('hrqk,khd->qhrd', grad_logit, key_tiles) * score_scale).astype(jnp.bfloat16).reshape(rows, QW)
    grad_keys = (jnp.einsum('hrqk,qhrd->khd', grad_logit, query_tiles) * score_scale).astype(jnp.bfloat16).reshape(rows, KW)
    grad_values = jnp.einsum('hrqk,qhrd->khd', rounded_prob, grad_tiles).astype(jnp.bfloat16).reshape(rows, KW)
    return (output, grad_queries, grad_keys, grad_values, weight_partial)

def reference(queries, key_heads, value_heads, segment_ids, out_weight, grad_out):
    stacked = (queries.reshape(N_DP, GROUP, QW), key_heads.reshape(N_DP, GROUP, KW), value_heads.reshape(N_DP, GROUP, KW), segment_ids, grad_out.reshape(N_DP, GROUP, DOUT))

    def one_step(weight_sum, group_inputs):
        output, grad_queries, grad_keys, grad_values, weight_partial = attend_group(group_inputs[0], group_inputs[1], group_inputs[2], group_inputs[3], group_inputs[4], out_weight)
        return (weight_sum + weight_partial, (output, grad_queries, grad_keys, grad_values))
    weight_sum, results = lax.scan(one_step, jnp.zeros((QW, DOUT), jnp.float32), stacked)
    output = results[0].reshape(TOKENS, DOUT)
    grad_queries = results[1].reshape(TOKENS, QW)
    grad_keys = results[2].reshape(TOKENS, KW)
    grad_values = results[3].reshape(TOKENS, KW)
    return (output, grad_queries, grad_keys, grad_values, weight_sum)
```

```python
import math

import jax
import jax.numpy as jnp
from jax import lax
from jax.sharding import PartitionSpec as P

HQ = 24
HK = 4
HD = 128


def per_device(queries, key_heads, value_heads, segment_ids, out_weight, grad_out):
    rows = queries.shape[0]
    n_cp = lax.axis_size("cp")
    group = rows * n_cp
    share = HQ // n_cp
    copies = n_cp // HK
    width = share * HD
    scale = 1.0 / math.sqrt(HD)
    f32 = jnp.float32
    bf16 = jnp.bfloat16
    weight_cols = lax.all_gather(out_weight, "dp", axis=0, tiled=True)
    packed = jnp.concatenate(
        [
            queries.reshape(rows, n_cp, width),
            jnp.repeat(key_heads.reshape(rows, HK, HD), copies, axis=1),
            jnp.repeat(value_heads.reshape(rows, HK, HD), copies, axis=1),
            jnp.broadcast_to(segment_ids[0].astype(bf16)[:, None, None], (rows, n_cp, HD)),
        ],
        axis=2,
    ).transpose(1, 0, 2)
    packed = lax.all_to_all(packed, "cp", 0, 0, tiled=True).reshape(group, -1)
    q = packed[:, :width].reshape(group, share, HD)
    k = packed[:, width : width + HD]
    v = packed[:, width + HD : width + 2 * HD]
    seg = packed[:, width + 2 * HD]
    pos = jnp.arange(group, dtype=jnp.int32)
    allowed = (seg[:, None] == seg[None, :]) & (pos[None, :] <= pos[:, None])
    logits = jnp.einsum("qrd,kd->rqk", q, k, preferred_element_type=f32) * scale
    logits = jnp.where(allowed, logits, -1e30)
    weights = jnp.exp(logits - jnp.max(logits, axis=-1, keepdims=True))
    weights = jnp.where(allowed, weights, 0.0)
    prob = weights / jnp.sum(weights, axis=-1, keepdims=True)
    rounded = prob.astype(bf16)
    attended = jnp.einsum("rqk,kd->qrd", rounded, v, preferred_element_type=f32)
    attended = attended.astype(bf16).reshape(group, width)
    attended_all = lax.all_gather(attended, "cp", axis=1, tiled=True)
    weight_partial = lax.dot_general(
        attended_all, grad_out, (((0,), (0,)), ((), ())), preferred_element_type=f32
    ).astype(bf16)
    grad_weight = lax.psum_scatter(weight_partial, "dp", scatter_dimension=0, tiled=True)
    part = lax.dot_general(
        grad_out, weight_cols, (((1,), (1,)), ((), ())), preferred_element_type=f32
    ).astype(bf16)
    ga = lax.psum_scatter(part, "cp", scatter_dimension=1, tiled=True)
    ga = ga.reshape(group, share, HD)
    grad_prob = jnp.einsum("qrd,kd->rqk", ga, v, preferred_element_type=f32)
    delta = jnp.sum(prob * grad_prob, axis=-1, keepdims=True)
    ds = (prob * (grad_prob - delta)).astype(bf16)
    dq = (jnp.einsum("rqk,kd->qrd", ds, k, preferred_element_type=f32) * scale).astype(bf16)
    dk = (jnp.einsum("rqk,qrd->kd", ds, q, preferred_element_type=f32) * scale).astype(bf16)
    dv = jnp.einsum("rqk,qrd->kd", rounded, ga, preferred_element_type=f32).astype(bf16)
    back = jnp.concatenate([dq.reshape(group, width), dk, dv], axis=1)
    back = lax.all_to_all(back.reshape(n_cp, rows, -1), "cp", 0, 0, tiled=True)
    back = back.transpose(1, 0, 2)
    summed = back[:, :, width:].reshape(rows, HK, copies, 2 * HD)
    summed = jnp.sum(summed.astype(f32), axis=2).astype(bf16)
    out = jnp.dot(attended_all, weight_cols, preferred_element_type=f32).astype(bf16)
    return (
        out,
        back[:, :, :width].reshape(rows, -1),
        summed[:, :, :HD].reshape(rows, -1),
        summed[:, :, HD:].reshape(rows, -1),
        grad_weight.astype(f32),
    )


def solution(mesh):
    rows = P(("dp", "cp"), None)
    grid = P("dp", "cp")
    return jax.shard_map(
        per_device,
        mesh=mesh,
        in_specs=(rows, rows, rows, grid, grid, grid),
        out_specs=(grid, rows, rows, rows, grid),
        check_vma=False,
    )
```

```python
import functools
import math

import jax
import jax.numpy as jnp
from jax import lax
from jax.experimental import pallas as pl
from jax.experimental.pallas import tpu as pltpu
from jax.sharding import PartitionSpec as P

HQ = 24
HK = 4
HD = 128
SCALE = 1.0 / math.sqrt(HD)
MESH = pl.DeviceIdType.MESH
F32 = jnp.float32
BF16 = jnp.bfloat16


def dot_nt(a, b):
    return lax.dot_general(a, b, (((1,), (1,)), ((), ())), preferred_element_type=F32)


def dot_tn(a, b):
    return lax.dot_general(a, b, (((0,), (0,)), ((), ())), preferred_element_type=F32)


def dot_nn(a, b):
    return jnp.dot(a, b, preferred_element_type=F32)


def kernel(
    n_dp, n_cp,
    q_ref, k_ref, v_ref, seg_ref, w_ref, go_ref,
    out_ref, dq_ref, dk_ref, dv_ref, dw_ref,
    qh, kh, vh, sg, bias, w_all, att, wp, sib, fr, fl, gas, gar, gsum, dqs, dqr, dka, dva, kvs, kvr,
    in_s, in_r, wr_s, wr_r, wl_s, wl_r, ws_s, ws_r, att_s, att_r, ga_s, ga_r,
    sb_s, sb_r, fr_s, fr_r, fl_s, fl_r, dq_s, dq_r, kv_s, kv_r,
):
    d = lax.axis_index("dp")
    c = lax.axis_index("cp")
    nz = n_dp // 2
    z = d // 2
    core = lax.rem(d, 2)
    sibling = d + 1 - 2 * core
    rows = q_ref.shape[0]
    group = rows * n_cp
    width = q_ref.shape[1] // n_cp
    share = width // HD
    copies = n_cp // HK
    shard, cols = w_ref.shape
    has_left = z > 0
    has_right = z < nz - 1
    pending = []

    def remote(src, dst, send, recv, dp, cp):
        return pltpu.make_async_remote_copy(
            src_ref=src, dst_ref=dst, send_sem=send, recv_sem=recv,
            device_id=(dp, cp), device_id_type=MESH,
        )

    def start(cond, make):
        pending.append((cond, make))
        if cond is None:
            make().start()
        else:
            pl.when(cond)(lambda: make().start())

    def wait_recv(cond, make):
        if cond is None:
            make().wait_recv()
        else:
            pl.when(cond)(lambda: make().wait_recv())

    barrier = pltpu.get_barrier_semaphore()

    def greet(dp, cp):
        pl.semaphore_signal(barrier, inc=1, device_id=(dp, cp), device_id_type=MESH)

    for j in range(1, n_cp):
        greet(d, lax.rem(c + j, n_cp))
    greet(sibling, c)
    pl.when(has_left)(lambda: greet(d - 2, c))
    pl.when(has_right)(lambda: greet(d + 2, c))
    pl.semaphore_wait(barrier, n_cp + jnp.where(has_left, 1, 0) + jnp.where(has_right, 1, 0))

    def w_right(s):
        slot = jnp.maximum(2 * (z - s) + core, 0)
        return remote(w_all.at[slot], w_all.at[slot], wr_s.at[s], wr_r.at[s], d + 2, c)

    def w_left(s):
        slot = jnp.minimum(2 * (z + s) + core, n_dp - 1)
        return remote(w_all.at[slot], w_all.at[slot], wl_s.at[s], wl_r.at[s], d - 2, c)

    def w_sib(slot, i):
        return remote(w_all.at[slot], w_all.at[slot], ws_s.at[i], ws_r.at[i], sibling, c)

    def row_slice(b):
        return pl.ds(pl.multiple_of(b * rows, rows), rows)

    def in_copies(j):
        peer = lax.rem(c + j, n_cp)
        qc = pl.ds(pl.multiple_of(peer * width, HD), width)
        kc = pl.ds(pl.multiple_of((peer // copies) * HD, HD), HD)
        mine = row_slice(c)
        pairs = (
            (q_ref.at[:, qc], qh.at[mine]),
            (k_ref.at[:, kc], kh.at[mine]),
            (v_ref.at[:, kc], vh.at[mine]),
            (seg_ref, sg.at[c]),
        )
        return [
            functools.partial(remote, a, b, in_s.at[i, j], in_r.at[i, j], d, peer)
            for i, (a, b) in enumerate(pairs)
        ]

    for j in range(1, n_cp):
        for make in in_copies(j):
            start(None, make)
    w_all[d] = w_ref[...]
    start(has_right, functools.partial(w_right, 0))
    start(has_left, functools.partial(w_left, 0))
    start(None, functools.partial(w_sib, d, 0))

    own_q = pl.ds(pl.multiple_of(c * width, HD), width)
    own_k = pl.ds(pl.multiple_of((c // copies) * HD, HD), HD)
    qh[row_slice(c), :] = q_ref[:, own_q]
    kh[row_slice(c), :] = k_ref[:, own_k]
    vh[row_slice(c), :] = v_ref[:, own_k]
    sg[c] = seg_ref[...]

    def ga_copy(t):
        return remote(
            gas.at[t], gar.at[c], ga_s.at[t], ga_r.at[lax.rem(t - c + n_cp, n_cp)], d, t
        )

    def ga_unit(t):
        def body(b, carry):
            unit = w_all[pl.ds(2 * t, 2)].reshape(2 * shard, cols)
            gas[t, row_slice(b), :] = dot_nt(go_ref[row_slice(b), :], unit).astype(BF16)
            return carry

        lax.fori_loop(0, n_cp, body, 0)

        @pl.when(t == c)
        def _():
            gar[c] = gas[t]

        @pl.when(t != c)
        def _():
            ga_copy(t).start()

    def gather_step(s):
        left_on, right_on = z - 1 - s >= 0, z + 1 + s < nz
        wait_recv(left_on, functools.partial(w_right, s))
        wait_recv(right_on, functools.partial(w_left, s))
        if s + 1 < nz - 1:
            start(left_on & has_right, functools.partial(w_right, s + 1))
            start(right_on & has_left, functools.partial(w_left, s + 1))
        lslot = jnp.maximum(2 * (z - 1 - s) + core, 0)
        rslot = jnp.minimum(2 * (z + 1 + s) + core, n_dp - 1)
        start(left_on, functools.partial(w_sib, lslot, 1 + s))
        start(right_on, functools.partial(w_sib, rslot, nz + s))

    def gather_use(s):
        for on, i, t in ((z - 1 - s >= 0, 1 + s, z - 1 - s), (z + 1 + s < nz, nz + s, z + 1 + s)):

            @pl.when(on)
            def _(i=i, t=t):
                w_sib(d, i).wait_recv()
                ga_unit(t)

    for j in range(1, n_cp):
        for make in in_copies(j):
            wait_recv(None, make)

    ones = jnp.ones((8, HD), BF16)
    for b in range(n_cp):
        at = slice(b * rows, (b + 1) * rows)
        seg_col = dot_tn(sg[b].astype(F32).astype(BF16), ones)[:, :1] * 0.125
        seg_row = jnp.concatenate([sg[e][:1, :] for e in range(n_cp)], axis=1).astype(F32)
        i = lax.broadcasted_iota(jnp.int32, (rows, group), 0) + b * rows
        jj = lax.broadcasted_iota(jnp.int32, (rows, group), 1)
        bias[at, :] = jnp.where((jj <= i) & (seg_col == seg_row), 0.0, -1e30)

    def probability(b, col):
        last = (b + 1) * rows
        q = qh[b * rows : last, col]
        s = dot_nt(q, kh[:last, :]) * SCALE + bias[b * rows : last, :last]
        e = jnp.exp(s - jnp.max(s, axis=1, keepdims=True))
        return q, e / jnp.sum(e, axis=1, keepdims=True)

    def head_col(r):
        return pl.ds(pl.multiple_of(r * HD, HD), HD)

    def forward(b):
        def body(r, carry):
            col = head_col(r)
            _, p = probability(b, col)
            a = dot_nn(p.astype(BF16), vh[: (b + 1) * rows, :]).astype(BF16)
            att[c, b * rows : (b + 1) * rows, col] = a
            return carry

        lax.fori_loop(0, share, body, 0)

    half = group // 2

    def att_copy(j, h):
        part = att.at[c, pl.ds(h * half, half)]
        return remote(part, part, att_s.at[h, j], att_r.at[h, j], d, lax.rem(c + j, n_cp))

    for h in range(2):
        for b in range(h * n_cp // 2, (h + 1) * n_cp // 2):
            forward(b)
        for j in range(1, n_cp):
            start(None, functools.partial(att_copy, j, h))
        if h == 0:
            gather_step(0)
    w_sib(d, 0).wait_recv()
    ga_unit(z)
    gather_use(0)
    if nz > 2:
        gather_step(1)

    def sib_copy(t):
        return remote(
            wp.at[2 * t + 1 - core], sib.at[t], sb_s.at[t], sb_r.at[t], sibling, c
        )

    def weight_unit(j, carry):
        t = lax.rem(c - j + n_cp, n_cp)

        @pl.when(j > 0)
        def _():
            att_copy(j, 0).wait_recv()
            att_copy(j, 1).wait_recv()

        part = dot_tn(att[t], go_ref[...]).astype(BF16)
        wp[pl.ds(2 * t, 2)] = part.reshape(2, shard, cols)
        sib_copy(t).start()
        return carry

    lax.fori_loop(0, n_cp, weight_unit, 0)

    def right_copy(s):
        t = nz - 1 - s
        return remote(wp.at[2 * t + core], fr.at[s], fr_s.at[s], fr_r.at[s], d + 2, c)

    def left_copy(s):
        return remote(wp.at[2 * s + core], fl.at[s], fl_s.at[s], fl_r.at[s], d - 2, c)

    def reduce_step(s):
        for t, on, has, make, arrived in (
            (nz - 1 - s, z < nz - 1 - s, has_left, right_copy, fr),
            (s, z > s, has_right, left_copy, fl),
        ):

            @pl.when(on)
            def _(t=t, has=has, make=make, arrived=arrived):
                sib_copy(t).wait_recv()
                mine = 2 * t + core

                @pl.when(has)
                def _():
                    make(s).wait_recv()
                    total = wp[mine].astype(F32) + sib[t].astype(F32) + arrived[s].astype(F32)
                    wp[mine] = total.astype(BF16)

                @pl.when(jnp.logical_not(has))
                def _():
                    wp[mine] = (wp[mine].astype(F32) + sib[t].astype(F32)).astype(BF16)

                make(s).start()

            pending.append((on, functools.partial(make, s)))

    for s in range(nz - 1):
        reduce_step(s)
        if s == 0:
            if nz > 2:
                gather_use(1)
            for e in range(2, nz - 1):
                gather_step(e)
                gather_use(e)
        if s == 1:
            output(n_cp, att, w_all, out_ref, row_slice, shard, cols)

    for j in range(1, n_cp):
        peer = lax.rem(c + j, n_cp)
        remote(gas.at[peer], gar.at[c], ga_s.at[peer], ga_r.at[j], d, peer).wait_recv()

    def sum_ga(b, carry):
        at = row_slice(b)
        total = gar[0, at, :].astype(F32)
        for e in range(1, n_cp):
            total = total + gar[e, at, :].astype(F32)
        gsum[at, :] = total.astype(BF16)
        return carry

    lax.fori_loop(0, n_cp, sum_ga, 0)
    dka[...] = jnp.zeros_like(dka)
    dva[...] = jnp.zeros_like(dva)

    def dq_copy(b):
        return remote(
            dqs.at[b], dqr.at[c], dq_s.at[b], dq_r.at[lax.rem(b - c + n_cp, n_cp)], d, b
        )

    def kv_copy(b):
        return remote(
            kvs.at[b], kvr.at[c], kv_s.at[b], kv_r.at[lax.rem(b - c + n_cp, n_cp)], d, b
        )

    def send_back(b, source, target, make):
        @pl.when(c == b)
        def _():
            target[c] = source[b]

        start(c != b, functools.partial(make, b))

    for b in reversed(range(n_cp)):
        last = (b + 1) * rows

        def body(r, carry, b=b, last=last):
            col = head_col(r)
            q, p = probability(b, col)
            g = gsum[b * rows : last, col]
            gp = dot_nt(g, vh[:last, :])
            delta = jnp.sum(p * gp, axis=1, keepdims=True)
            ds = (p * (gp - delta)).astype(BF16)
            dqs[b, :, col] = (dot_nn(ds, kh[:last, :]) * SCALE).astype(BF16)
            dka[:last, :] += dot_tn(ds, q)
            dva[:last, :] += dot_tn(p.astype(BF16), g)
            return carry

        lax.fori_loop(0, share, body, 0)
        send_back(b, dqs, dqr, dq_copy)
    for b in range(n_cp):
        at = slice(b * rows, (b + 1) * rows)
        kvs[b, :, :HD] = (dka[at, :] * SCALE).astype(BF16)
        kvs[b, :, HD:] = dva[at, :].astype(BF16)
        send_back(b, kvs, kvr, kv_copy)

    sib_copy(z).wait_recv()
    dw_ref[...] = wp[2 * z + core].astype(F32) + sib[z].astype(F32)

    @pl.when(has_left)
    def _():
        s = jnp.minimum(nz - 1 - z, nz - 2)
        remote(wp.at[d], fr.at[s], fr_s.at[s], fr_r.at[s], d + 2, c).wait_recv()
        dw_ref[...] += fr[s].astype(F32)

    @pl.when(has_right)
    def _():
        s = jnp.minimum(z, nz - 2)
        remote(wp.at[d], fl.at[s], fl_s.at[s], fl_r.at[s], d - 2, c).wait_recv()
        dw_ref[...] += fl[s].astype(F32)

    for j in range(1, n_cp):
        peer = lax.rem(c + j, n_cp)
        remote(dqs.at[peer], dqr.at[c], dq_s.at[peer], dq_r.at[j], d, peer).wait_recv()
        remote(kvs.at[peer], kvr.at[c], kv_s.at[peer], kv_r.at[j], d, peer).wait_recv()
    for e in range(n_cp):
        dq_ref[:, e * width : (e + 1) * width] = dqr[e]
    for h in range(HK):
        total = kvr[h * copies].astype(F32)
        for e in range(1, copies):
            total = total + kvr[h * copies + e].astype(F32)
        dk_ref[:, h * HD : (h + 1) * HD] = total[:, :HD].astype(BF16)
        dv_ref[:, h * HD : (h + 1) * HD] = total[:, HD:].astype(BF16)

    for cond, make in pending:
        if cond is None:
            make().wait_send()
        else:
            pl.when(cond)(functools.partial(lambda m: m().wait_send(), make))
    for t in range(n_cp):
        pl.when(c != t)(functools.partial(lambda t: ga_copy(t).wait_send(), t))
        sib_copy(t).wait_send()


def output(n_cp, att, w_all, out_ref, row_slice, shard, cols):
    def body(b, carry):
        at = row_slice(b)
        total = jnp.zeros((out_ref.shape[0] // n_cp, cols), F32)
        for t in range(n_cp):
            unit = w_all[2 * t : 2 * t + 2].reshape(2 * shard, cols)
            total = total + dot_nn(att[t, at, :], unit)
        out_ref[at, :] = total.astype(BF16)
        return carry

    lax.fori_loop(0, n_cp, body, 0)


def per_device(n_dp, n_cp, queries, key_heads, value_heads, segment_ids, out_weight, grad_out):
    rows = queries.shape[0]
    group = rows * n_cp
    width = queries.shape[1] // n_cp
    shard, cols = out_weight.shape
    nz = n_dp // 2
    segments = jnp.broadcast_to(segment_ids, (8, rows))
    vmem = pl.BlockSpec(memory_space=pltpu.VMEM)
    dma = pltpu.SemaphoreType.DMA
    block = jax.ShapeDtypeStruct
    return pl.pallas_call(
        functools.partial(kernel, n_dp, n_cp),
        out_shape=(
            block((group, cols), BF16),
            block(queries.shape, BF16),
            block(key_heads.shape, BF16),
            block(value_heads.shape, BF16),
            block((shard, cols), F32),
        ),
        in_specs=[vmem] * 6,
        out_specs=[vmem] * 5,
        scratch_shapes=[
            pltpu.VMEM((group, width), BF16),
            pltpu.VMEM((group, HD), BF16),
            pltpu.VMEM((group, HD), BF16),
            pltpu.VMEM((n_cp, 8, rows), jnp.int32),
            pltpu.VMEM((group, group), F32),
            pltpu.VMEM((n_dp, shard, cols), BF16),
            pltpu.VMEM((n_cp, group, width), BF16),
            pltpu.VMEM((n_dp, shard, cols), BF16),
            pltpu.VMEM((nz, shard, cols), BF16),
            pltpu.VMEM((nz - 1, shard, cols), BF16),
            pltpu.VMEM((nz - 1, shard, cols), BF16),
            pltpu.VMEM((n_cp, group, width), BF16),
            pltpu.VMEM((n_cp, group, width), BF16),
            pltpu.VMEM((group, width), BF16),
            pltpu.VMEM((n_cp, rows, width), BF16),
            pltpu.VMEM((n_cp, rows, width), BF16),
            pltpu.VMEM((group, HD), F32),
            pltpu.VMEM((group, HD), F32),
            pltpu.VMEM((n_cp, rows, 2 * HD), BF16),
            pltpu.VMEM((n_cp, rows, 2 * HD), BF16),
            dma((4, n_cp)), dma((4, n_cp)),
            dma((nz - 1,)), dma((nz - 1,)), dma((nz - 1,)), dma((nz - 1,)),
            dma((2 * nz - 1,)), dma((2 * nz - 1,)),
            dma((2, n_cp)), dma((2, n_cp)),
            dma((n_cp,)), dma((n_cp,)),
            dma((nz,)), dma((nz,)),
            dma((nz - 1,)), dma((nz - 1,)), dma((nz - 1,)), dma((nz - 1,)),
            dma((n_cp,)), dma((n_cp,)), dma((n_cp,)), dma((n_cp,)),
        ],
        compiler_params=pltpu.CompilerParams(
            collective_id=0, has_side_effects=True, vmem_limit_bytes=60 * 1024 * 1024
        ),
    )(queries, key_heads, value_heads, segments, out_weight, grad_out)


def solution(mesh):
    rows = P(("dp", "cp"), None)
    grid = P("dp", "cp")
    return jax.shard_map(
        functools.partial(per_device, mesh.shape["dp"], mesh.shape["cp"]),
        mesh=mesh,
        in_specs=(rows, rows, rows, grid, grid, grid),
        out_specs=(grid, rows, rows, rows, grid),
        check_vma=False,
    )
```

```python
import functools
import math

import jax
import jax.numpy as jnp
from jax import lax
from jax.experimental import pallas as pl
from jax.experimental.pallas import tpu as pltpu
from jax.sharding import PartitionSpec as P

HQ = 24
HK = 4
HD = 128
SCALE = 1.0 / math.sqrt(HD)
MESH = pl.DeviceIdType.MESH
F32 = jnp.float32
BF16 = jnp.bfloat16


def dot_nt(a, b):
    return lax.dot_general(a, b, (((1,), (1,)), ((), ())), preferred_element_type=F32)


def dot_tn(a, b):
    return lax.dot_general(a, b, (((0,), (0,)), ((), ())), preferred_element_type=F32)


def dot_nn(a, b):
    return jnp.dot(a, b, preferred_element_type=F32)


def kernel(
    n_dp, n_cp,
    q_ref, k_ref, v_ref, seg_ref, w_ref, go_ref,
    out_ref, dq_ref, dk_ref, dv_ref, dw_ref,
    qh, kh, vh, sg, bias, w_all, att, wp, sib, fr, fl, gas, gar, gsum, dqs, dqr, dka, dva, kvs, kvr,
    in_s, in_r, wr_s, wr_r, wl_s, wl_r, ws_s, ws_r, att_s, att_r, ga_s, ga_r,
    sb_s, sb_r, fr_s, fr_r, fl_s, fl_r, dq_s, dq_r, kv_s, kv_r,
):
    d = lax.axis_index("dp")
    c = lax.axis_index("cp")
    nz = n_dp // 2
    z = d // 2
    core = lax.rem(d, 2)
    sibling = d + 1 - 2 * core
    rows = q_ref.shape[0]
    group = rows * n_cp
    width = q_ref.shape[1] // n_cp
    share = width // HD
    copies = n_cp // HK
    shard, cols = w_ref.shape
    has_left = z > 0
    has_right = z < nz - 1
    pending = []

    def remote(src, dst, send, recv, dp, cp):
        return pltpu.make_async_remote_copy(
            src_ref=src, dst_ref=dst, send_sem=send, recv_sem=recv,
            device_id=(dp, cp), device_id_type=MESH,
        )

    def start(cond, make):
        pending.append((cond, make))
        if cond is None:
            make().start()
        else:
            pl.when(cond)(lambda: make().start())

    def wait_recv(cond, make):
        if cond is None:
            make().wait_recv()
        else:
            pl.when(cond)(lambda: make().wait_recv())

    barrier = pltpu.get_barrier_semaphore()

    def greet(dp, cp):
        pl.semaphore_signal(barrier, inc=1, device_id=(dp, cp), device_id_type=MESH)

    for j in range(1, n_cp):
        greet(d, lax.rem(c + j, n_cp))
    greet(sibling, c)
    pl.when(has_left)(lambda: greet(d - 2, c))
    pl.when(has_right)(lambda: greet(d + 2, c))
    pl.semaphore_wait(barrier, n_cp + jnp.where(has_left, 1, 0) + jnp.where(has_right, 1, 0))

    def w_right(s):
        slot = jnp.maximum(2 * (z - s) + core, 0)
        return remote(w_all.at[slot], w_all.at[slot], wr_s.at[s], wr_r.at[s], d + 2, c)

    def w_left(s):
        slot = jnp.minimum(2 * (z + s) + core, n_dp - 1)
        return remote(w_all.at[slot], w_all.at[slot], wl_s.at[s], wl_r.at[s], d - 2, c)

    def w_sib(slot, i):
        return remote(w_all.at[slot], w_all.at[slot], ws_s.at[i], ws_r.at[i], sibling, c)

    def row_slice(b):
        return pl.ds(pl.multiple_of(b * rows, rows), rows)

    def in_copies(j):
        peer = lax.rem(c + j, n_cp)
        qc = pl.ds(pl.multiple_of(peer * width, HD), width)
        kc = pl.ds(pl.multiple_of((peer // copies) * HD, HD), HD)
        mine = row_slice(c)
        pairs = (
            (q_ref.at[:, qc], qh.at[mine]),
            (k_ref.at[:, kc], kh.at[mine]),
            (v_ref.at[:, kc], vh.at[mine]),
            (seg_ref, sg.at[c]),
        )
        return [
            functools.partial(remote, a, b, in_s.at[i, j], in_r.at[i, j], d, peer)
            for i, (a, b) in enumerate(pairs)
        ]

    for j in range(1, n_cp):
        for make in in_copies(j):
            start(None, make)
    w_all[d] = w_ref[...]
    start(has_right, functools.partial(w_right, 0))
    start(has_left, functools.partial(w_left, 0))
    start(None, functools.partial(w_sib, d, 0))

    own_q = pl.ds(pl.multiple_of(c * width, HD), width)
    own_k = pl.ds(pl.multiple_of((c // copies) * HD, HD), HD)
    qh[row_slice(c), :] = q_ref[:, own_q]
    kh[row_slice(c), :] = k_ref[:, own_k]
    vh[row_slice(c), :] = v_ref[:, own_k]
    sg[c] = seg_ref[...]

    def ga_copy(t):
        return remote(
            gas.at[t], gar.at[c], ga_s.at[t], ga_r.at[lax.rem(t - c + n_cp, n_cp)], d, t
        )

    def ga_unit(t):
        def body(b, carry):
            unit = w_all[pl.ds(2 * t, 2)].reshape(2 * shard, cols)
            gas[t, row_slice(b), :] = dot_nt(go_ref[row_slice(b), :], unit).astype(BF16)
            return carry

        lax.fori_loop(0, n_cp, body, 0)

        @pl.when(t == c)
        def _():
            gar[c] = gas[t]

        @pl.when(t != c)
        def _():
            ga_copy(t).start()

    def gather_step(s):
        left_on, right_on = z - 1 - s >= 0, z + 1 + s < nz
        wait_recv(left_on, functools.partial(w_right, s))
        wait_recv(right_on, functools.partial(w_left, s))
        if s + 1 < nz - 1:
            start(left_on & has_right, functools.partial(w_right, s + 1))
            start(right_on & has_left, functools.partial(w_left, s + 1))
        lslot = jnp.maximum(2 * (z - 1 - s) + core, 0)
        rslot = jnp.minimum(2 * (z + 1 + s) + core, n_dp - 1)
        start(left_on, functools.partial(w_sib, lslot, 1 + s))
        start(right_on, functools.partial(w_sib, rslot, nz + s))

    def gather_use(s):
        for on, i, t in ((z - 1 - s >= 0, 1 + s, z - 1 - s), (z + 1 + s < nz, nz + s, z + 1 + s)):

            @pl.when(on)
            def _(i=i, t=t):
                w_sib(d, i).wait_recv()
                ga_unit(t)

    for j in range(1, n_cp):
        for make in in_copies(j):
            wait_recv(None, make)

    ones = jnp.ones((8, HD), BF16)
    for b in range(n_cp):
        at = slice(b * rows, (b + 1) * rows)
        seg_col = dot_tn(sg[b].astype(F32).astype(BF16), ones)[:, :1] * 0.125
        seg_row = jnp.concatenate([sg[e][:1, :] for e in range(n_cp)], axis=1).astype(F32)
        i = lax.broadcasted_iota(jnp.int32, (rows, group), 0) + b * rows
        jj = lax.broadcasted_iota(jnp.int32, (rows, group), 1)
        bias[at, :] = jnp.where((jj <= i) & (seg_col == seg_row), 0.0, -1e30)

    def probability(b, col):
        last = (b + 1) * rows
        q = qh[b * rows : last, col]
        s = dot_nt(q, kh[:last, :]) * SCALE + bias[b * rows : last, :last]
        e = jnp.exp(s - jnp.max(s, axis=1, keepdims=True))
        return q, e / jnp.sum(e, axis=1, keepdims=True)

    def head_col(r):
        return pl.ds(pl.multiple_of(r * HD, HD), HD)

    def forward(b):
        def body(r, carry):
            col = head_col(r)
            _, p = probability(b, col)
            a = dot_nn(p.astype(BF16), vh[: (b + 1) * rows, :]).astype(BF16)
            att[c, b * rows : (b + 1) * rows, col] = a
            return carry

        lax.fori_loop(0, share, body, 0)

    half = group // 2

    def att_copy(j, h):
        part = att.at[c, pl.ds(h * half, half)]
        return remote(part, part, att_s.at[h, j], att_r.at[h, j], d, lax.rem(c + j, n_cp))

    for h in range(2):
        for b in range(h * n_cp // 2, (h + 1) * n_cp // 2):
            forward(b)
        for j in range(1, n_cp):
            start(None, functools.partial(att_copy, j, h))
        if h == 0:
            gather_step(0)
    w_sib(d, 0).wait_recv()
    ga_unit(z)
    gather_use(0)
    if nz > 2:
        gather_step(1)
        gather_use(1)

    def sib_copy(t):
        return remote(
            wp.at[2 * t + 1 - core], sib.at[t], sb_s.at[t], sb_r.at[t], sibling, c
        )

    def weight_unit(j, carry):
        t = lax.rem(c - j + n_cp, n_cp)

        @pl.when(j > 0)
        def _():
            att_copy(j, 0).wait_recv()
            att_copy(j, 1).wait_recv()

        part = dot_tn(att[t], go_ref[...]).astype(BF16)
        wp[pl.ds(2 * t, 2)] = part.reshape(2, shard, cols)
        sib_copy(t).start()
        return carry

    lax.fori_loop(0, n_cp, weight_unit, 0)

    def right_copy(s):
        t = nz - 1 - s
        return remote(wp.at[2 * t + core], fr.at[s], fr_s.at[s], fr_r.at[s], d + 2, c)

    def left_copy(s):
        return remote(wp.at[2 * s + core], fl.at[s], fl_s.at[s], fl_r.at[s], d - 2, c)

    def reduce_step(time):
        right, left = time - z, time - (nz - 1 - z)
        for s, t, has, make, arrived in (
            (right, nz - 1 - right, has_left, right_copy, fr),
            (left, left, has_right, left_copy, fl),
        ):

            @pl.when(s >= 0)
            def _(s=s, t=t, has=has, make=make, arrived=arrived):
                sib_copy(t).wait_recv()
                mine = 2 * t + core

                @pl.when(has)
                def _():
                    make(s).wait_recv()
                    total = wp[mine].astype(F32) + sib[t].astype(F32) + arrived[s].astype(F32)
                    wp[mine] = total.astype(BF16)

                @pl.when(jnp.logical_not(has))
                def _():
                    wp[mine] = (wp[mine].astype(F32) + sib[t].astype(F32)).astype(BF16)

                make(s).start()

            pending.append((s >= 0, functools.partial(make, s)))

    reduce_step(0)
    for e in range(2, nz - 1):
        gather_step(e)
        gather_use(e)
    for time in range(1, nz - 1):
        reduce_step(time)
        if time == 1:
            output(n_cp, att, w_all, out_ref, row_slice, shard, cols)

    for j in range(1, n_cp):
        peer = lax.rem(c + j, n_cp)
        remote(gas.at[peer], gar.at[c], ga_s.at[peer], ga_r.at[j], d, peer).wait_recv()

    def sum_ga(b, carry):
        at = row_slice(b)
        total = gar[0, at, :].astype(F32)
        for e in range(1, n_cp):
            total = total + gar[e, at, :].astype(F32)
        gsum[at, :] = total.astype(BF16)
        return carry

    lax.fori_loop(0, n_cp, sum_ga, 0)
    dka[...] = jnp.zeros_like(dka)
    dva[...] = jnp.zeros_like(dva)

    def dq_copy(b):
        return remote(
            dqs.at[b], dqr.at[c], dq_s.at[b], dq_r.at[lax.rem(b - c + n_cp, n_cp)], d, b
        )

    def kv_copy(b):
        return remote(
            kvs.at[b], kvr.at[c], kv_s.at[b], kv_r.at[lax.rem(b - c + n_cp, n_cp)], d, b
        )

    def send_back(b, source, target, make):
        @pl.when(c == b)
        def _():
            target[c] = source[b]

        start(c != b, functools.partial(make, b))

    for b in reversed(range(n_cp)):
        last = (b + 1) * rows

        def body(r, carry, b=b, last=last):
            col = head_col(r)
            q, p = probability(b, col)
            g = gsum[b * rows : last, col]
            gp = dot_nt(g, vh[:last, :])
            delta = jnp.sum(p * gp, axis=1, keepdims=True)
            ds = (p * (gp - delta)).astype(BF16)
            dqs[b, :, col] = (dot_nn(ds, kh[:last, :]) * SCALE).astype(BF16)
            dka[:last, :] += dot_tn(ds, q)
            dva[:last, :] += dot_tn(p.astype(BF16), g)
            return carry

        lax.fori_loop(0, share, body, 0)
        send_back(b, dqs, dqr, dq_copy)
    for b in range(n_cp):
        at = slice(b * rows, (b + 1) * rows)
        kvs[b, :, :HD] = (dka[at, :] * SCALE).astype(BF16)
        kvs[b, :, HD:] = dva[at, :].astype(BF16)
        send_back(b, kvs, kvr, kv_copy)

    sib_copy(z).wait_recv()
    dw_ref[...] = wp[2 * z + core].astype(F32) + sib[z].astype(F32)

    @pl.when(has_left)
    def _():
        s = jnp.minimum(nz - 1 - z, nz - 2)
        remote(wp.at[d], fr.at[s], fr_s.at[s], fr_r.at[s], d + 2, c).wait_recv()
        dw_ref[...] += fr[s].astype(F32)

    @pl.when(has_right)
    def _():
        s = jnp.minimum(z, nz - 2)
        remote(wp.at[d], fl.at[s], fl_s.at[s], fl_r.at[s], d - 2, c).wait_recv()
        dw_ref[...] += fl[s].astype(F32)

    for j in range(1, n_cp):
        peer = lax.rem(c + j, n_cp)
        remote(dqs.at[peer], dqr.at[c], dq_s.at[peer], dq_r.at[j], d, peer).wait_recv()
        remote(kvs.at[peer], kvr.at[c], kv_s.at[peer], kv_r.at[j], d, peer).wait_recv()
    for e in range(n_cp):
        dq_ref[:, e * width : (e + 1) * width] = dqr[e]
    for h in range(HK):
        total = kvr[h * copies].astype(F32)
        for e in range(1, copies):
            total = total + kvr[h * copies + e].astype(F32)
        dk_ref[:, h * HD : (h + 1) * HD] = total[:, :HD].astype(BF16)
        dv_ref[:, h * HD : (h + 1) * HD] = total[:, HD:].astype(BF16)

    for cond, make in pending:
        if cond is None:
            make().wait_send()
        else:
            pl.when(cond)(functools.partial(lambda m: m().wait_send(), make))
    for t in range(n_cp):
        pl.when(c != t)(functools.partial(lambda t: ga_copy(t).wait_send(), t))
        sib_copy(t).wait_send()


def output(n_cp, att, w_all, out_ref, row_slice, shard, cols):
    def body(b, carry):
        at = row_slice(b)
        total = jnp.zeros((out_ref.shape[0] // n_cp, cols), F32)
        for t in range(n_cp):
            unit = w_all[2 * t : 2 * t + 2].reshape(2 * shard, cols)
            total = total + dot_nn(att[t, at, :], unit)
        out_ref[at, :] = total.astype(BF16)
        return carry

    lax.fori_loop(0, n_cp, body, 0)


def per_device(n_dp, n_cp, queries, key_heads, value_heads, segment_ids, out_weight, grad_out):
    rows = queries.shape[0]
    group = rows * n_cp
    width = queries.shape[1] // n_cp
    shard, cols = out_weight.shape
    nz = n_dp // 2
    segments = jnp.broadcast_to(segment_ids, (8, rows))
    vmem = pl.BlockSpec(memory_space=pltpu.VMEM)
    dma = pltpu.SemaphoreType.DMA
    block = jax.ShapeDtypeStruct
    return pl.pallas_call(
        functools.partial(kernel, n_dp, n_cp),
        out_shape=(
            block((group, cols), BF16),
            block(queries.shape, BF16),
            block(key_heads.shape, BF16),
            block(value_heads.shape, BF16),
            block((shard, cols), F32),
        ),
        in_specs=[vmem] * 6,
        out_specs=[vmem] * 5,
        scratch_shapes=[
            pltpu.VMEM((group, width), BF16),
            pltpu.VMEM((group, HD), BF16),
            pltpu.VMEM((group, HD), BF16),
            pltpu.VMEM((n_cp, 8, rows), jnp.int32),
            pltpu.VMEM((group, group), F32),
            pltpu.VMEM((n_dp, shard, cols), BF16),
            pltpu.VMEM((n_cp, group, width), BF16),
            pltpu.VMEM((n_dp, shard, cols), BF16),
            pltpu.VMEM((nz, shard, cols), BF16),
            pltpu.VMEM((nz - 1, shard, cols), BF16),
            pltpu.VMEM((nz - 1, shard, cols), BF16),
            pltpu.VMEM((n_cp, group, width), BF16),
            pltpu.VMEM((n_cp, group, width), BF16),
            pltpu.VMEM((group, width), BF16),
            pltpu.VMEM((n_cp, rows, width), BF16),
            pltpu.VMEM((n_cp, rows, width), BF16),
            pltpu.VMEM((group, HD), F32),
            pltpu.VMEM((group, HD), F32),
            pltpu.VMEM((n_cp, rows, 2 * HD), BF16),
            pltpu.VMEM((n_cp, rows, 2 * HD), BF16),
            dma((4, n_cp)), dma((4, n_cp)),
            dma((nz - 1,)), dma((nz - 1,)), dma((nz - 1,)), dma((nz - 1,)),
            dma((2 * nz - 1,)), dma((2 * nz - 1,)),
            dma((2, n_cp)), dma((2, n_cp)),
            dma((n_cp,)), dma((n_cp,)),
            dma((nz,)), dma((nz,)),
            dma((nz - 1,)), dma((nz - 1,)), dma((nz - 1,)), dma((nz - 1,)),
            dma((n_cp,)), dma((n_cp,)), dma((n_cp,)), dma((n_cp,)),
        ],
        compiler_params=pltpu.CompilerParams(
            collective_id=0, has_side_effects=True, vmem_limit_bytes=60 * 1024 * 1024
        ),
    )(queries, key_heads, value_heads, segments, out_weight, grad_out)


def solution(mesh):
    rows = P(("dp", "cp"), None)
    grid = P("dp", "cp")
    return jax.shard_map(
        functools.partial(per_device, mesh.shape["dp"], mesh.shape["cp"]),
        mesh=mesh,
        in_specs=(rows, rows, rows, grid, grid, grid),
        out_specs=(grid, rows, rows, rows, grid),
        check_vma=False,
    )
```

```python
import functools
import math

import jax
import jax.numpy as jnp
from jax import lax
from jax.experimental import pallas as pl
from jax.experimental.pallas import tpu as pltpu
from jax.sharding import PartitionSpec as P

HQ = 24
HK = 4
HD = 128
SCALE = 1.0 / math.sqrt(HD)
MESH = pl.DeviceIdType.MESH
F32 = jnp.float32
BF16 = jnp.bfloat16


def dot_nt(a, b):
    return lax.dot_general(a, b, (((1,), (1,)), ((), ())), preferred_element_type=F32)


def dot_tn(a, b):
    return lax.dot_general(a, b, (((0,), (0,)), ((), ())), preferred_element_type=F32)


def dot_nn(a, b):
    return jnp.dot(a, b, preferred_element_type=F32)


def kernel(
    n_dp, n_cp,
    q_ref, k_ref, v_ref, seg_ref, w_ref, go_ref,
    out_ref, dq_ref, dk_ref, dv_ref, dw_ref,
    qh, kh, vh, sg, bias, w_all, att, wp, sib, fr, fl, gas, gar, gsum, dqs, dqr, dka, dva, kvs, kvr, prob,
    in_s, in_r, wr_s, wr_r, wl_s, wl_r, ws_s, ws_r, att_s, att_r, ga_s, ga_r,
    sb_s, sb_r, fr_s, fr_r, fl_s, fl_r, dq_s, dq_r, kv_s, kv_r,
):
    d = lax.axis_index("dp")
    c = lax.axis_index("cp")
    nz = n_dp // 2
    z = d // 2
    core = lax.rem(d, 2)
    sibling = d + 1 - 2 * core
    rows = q_ref.shape[0]
    group = rows * n_cp
    width = q_ref.shape[1] // n_cp
    share = width // HD
    copies = n_cp // HK
    shard, cols = w_ref.shape
    has_left = z > 0
    has_right = z < nz - 1
    pending = []

    def remote(src, dst, send, recv, dp, cp):
        return pltpu.make_async_remote_copy(
            src_ref=src, dst_ref=dst, send_sem=send, recv_sem=recv,
            device_id=(dp, cp), device_id_type=MESH,
        )

    def start(cond, make):
        pending.append((cond, make))
        if cond is None:
            make().start()
        else:
            pl.when(cond)(lambda: make().start())

    def wait_recv(cond, make):
        if cond is None:
            make().wait_recv()
        else:
            pl.when(cond)(lambda: make().wait_recv())

    barrier = pltpu.get_barrier_semaphore()

    def greet(dp, cp):
        pl.semaphore_signal(barrier, inc=1, device_id=(dp, cp), device_id_type=MESH)

    for j in range(1, n_cp):
        greet(d, lax.rem(c + j, n_cp))
    greet(sibling, c)
    pl.when(has_left)(lambda: greet(d - 2, c))
    pl.when(has_right)(lambda: greet(d + 2, c))
    pl.semaphore_wait(barrier, n_cp + jnp.where(has_left, 1, 0) + jnp.where(has_right, 1, 0))

    def w_right(s):
        slot = jnp.maximum(2 * (z - s) + core, 0)
        return remote(w_all.at[slot], w_all.at[slot], wr_s.at[s], wr_r.at[s], d + 2, c)

    def w_left(s):
        slot = jnp.minimum(2 * (z + s) + core, n_dp - 1)
        return remote(w_all.at[slot], w_all.at[slot], wl_s.at[s], wl_r.at[s], d - 2, c)

    def w_sib(slot, i):
        return remote(w_all.at[slot], w_all.at[slot], ws_s.at[i], ws_r.at[i], sibling, c)

    def row_slice(b):
        return pl.ds(pl.multiple_of(b * rows, rows), rows)

    def in_copies(j):
        peer = lax.rem(c + j, n_cp)
        qc = pl.ds(pl.multiple_of(peer * width, HD), width)
        kc = pl.ds(pl.multiple_of((peer // copies) * HD, HD), HD)
        mine = row_slice(c)
        pairs = (
            (q_ref.at[:, qc], qh.at[mine]),
            (k_ref.at[:, kc], kh.at[mine]),
            (v_ref.at[:, kc], vh.at[mine]),
            (seg_ref, sg.at[c]),
        )
        return [
            functools.partial(remote, a, b, in_s.at[i, j], in_r.at[i, j], d, peer)
            for i, (a, b) in enumerate(pairs)
        ]

    for j in range(1, n_cp):
        for make in in_copies(j):
            start(None, make)
    w_all[d] = w_ref[...]
    start(has_right, functools.partial(w_right, 0))
    start(has_left, functools.partial(w_left, 0))
    start(None, functools.partial(w_sib, d, 0))

    own_q = pl.ds(pl.multiple_of(c * width, HD), width)
    own_k = pl.ds(pl.multiple_of((c // copies) * HD, HD), HD)
    qh[row_slice(c), :] = q_ref[:, own_q]
    kh[row_slice(c), :] = k_ref[:, own_k]
    vh[row_slice(c), :] = v_ref[:, own_k]
    sg[c] = seg_ref[...]

    half = group // 2
    half_blocks = n_cp // 2

    def ga_copy(t, h):
        part = pl.ds(h * half, half)
        j = lax.rem(t - c + n_cp, n_cp)
        return remote(gas.at[t, part], gar.at[c, part], ga_s.at[h, t], ga_r.at[h, j], d, t)

    def ga_unit(t):
        def body(b, carry):
            unit = w_all[pl.ds(2 * t, 2)].reshape(2 * shard, cols)
            gas[t, row_slice(b), :] = dot_nt(go_ref[row_slice(b), :], unit).astype(BF16)
            return carry

        for h in (1, 0):
            lax.fori_loop(h * half_blocks, (h + 1) * half_blocks, body, 0)

            @pl.when(t != c)
            def _(h=h):
                ga_copy(t, h).start()

        @pl.when(t == c)
        def _():
            gar[c] = gas[t]

    def gather_step(s):
        left_on, right_on = z - 1 - s >= 0, z + 1 + s < nz
        wait_recv(left_on, functools.partial(w_right, s))
        wait_recv(right_on, functools.partial(w_left, s))
        if s + 1 < nz - 1:
            start(left_on & has_right, functools.partial(w_right, s + 1))
            start(right_on & has_left, functools.partial(w_left, s + 1))
        lslot = jnp.maximum(2 * (z - 1 - s) + core, 0)
        rslot = jnp.minimum(2 * (z + 1 + s) + core, n_dp - 1)
        start(left_on, functools.partial(w_sib, lslot, 1 + s))
        start(right_on, functools.partial(w_sib, rslot, nz + s))

    def gather_use(s):
        for on, i, t in ((z - 1 - s >= 0, 1 + s, z - 1 - s), (z + 1 + s < nz, nz + s, z + 1 + s)):

            @pl.when(on)
            def _(i=i, t=t):
                w_sib(d, i).wait_recv()
                ga_unit(t)

    w_sib(d, 0).wait_recv()
    ga_unit(z)
    for j in range(1, n_cp):
        for make in in_copies(j):
            wait_recv(None, make)

    ones = jnp.ones((8, HD), BF16)
    for b in range(n_cp):
        at = slice(b * rows, (b + 1) * rows)
        seg_col = dot_tn(sg[b].astype(F32).astype(BF16), ones)[:, :1] * 0.125
        seg_row = jnp.concatenate([sg[e][:1, :] for e in range(n_cp)], axis=1).astype(F32)
        i = lax.broadcasted_iota(jnp.int32, (rows, group), 0) + b * rows
        jj = lax.broadcasted_iota(jnp.int32, (rows, group), 1)
        bias[at, :] = jnp.where((jj <= i) & (seg_col == seg_row), 0.0, -1e30)

    def probability(b, col):
        last = (b + 1) * rows
        q = qh[b * rows : last, col]
        s = dot_nt(q, kh[:last, :]) * SCALE + bias[b * rows : last, :last]
        e = jnp.exp(s - jnp.max(s, axis=1, keepdims=True))
        return e / jnp.sum(e, axis=1, keepdims=True)

    def head_col(r):
        return pl.ds(pl.multiple_of(r * HD, HD), HD)

    def forward(b):
        def body(r, carry):
            col = head_col(r)
            p = probability(b, col)
            prob[r, b * rows : (b + 1) * rows, : (b + 1) * rows] = p
            a = dot_nn(p.astype(BF16), vh[: (b + 1) * rows, :]).astype(BF16)
            att[c, b * rows : (b + 1) * rows, col] = a
            return carry

        lax.fori_loop(0, share, body, 0)

    def att_copy(j, h):
        part = att.at[c, pl.ds(h * half, half)]
        return remote(part, part, att_s.at[h, j], att_r.at[h, j], d, lax.rem(c + j, n_cp))

    for h in range(2):
        for b in range(h * n_cp // 2, (h + 1) * n_cp // 2):
            forward(b)
        for j in range(1, n_cp):
            start(None, functools.partial(att_copy, j, h))
        if h == 0:
            gather_step(0)
    gather_use(0)
    if nz > 2:
        gather_step(1)
        gather_use(1)

    def sib_copy(t):
        return remote(
            wp.at[2 * t + 1 - core], sib.at[t], sb_s.at[t], sb_r.at[t], sibling, c
        )

    def weight_unit(j, carry):
        t = lax.rem(c - j + n_cp, n_cp)

        @pl.when(j > 0)
        def _():
            att_copy(j, 0).wait_recv()
            att_copy(j, 1).wait_recv()

        part = dot_tn(att[t], go_ref[...]).astype(BF16)
        wp[pl.ds(2 * t, 2)] = part.reshape(2, shard, cols)
        sib_copy(t).start()
        return carry

    lax.fori_loop(0, n_cp, weight_unit, 0)

    def right_copy(s):
        t = nz - 1 - s
        return remote(wp.at[2 * t + core], fr.at[s], fr_s.at[s], fr_r.at[s], d + 2, c)

    def left_copy(s):
        return remote(wp.at[2 * s + core], fl.at[s], fl_s.at[s], fl_r.at[s], d - 2, c)

    def reduce_step(time):
        right, left = time - z, time - (nz - 1 - z)
        for s, t, has, make, arrived in (
            (right, nz - 1 - right, has_left, right_copy, fr),
            (left, left, has_right, left_copy, fl),
        ):

            @pl.when(s >= 0)
            def _(s=s, t=t, has=has, make=make, arrived=arrived):
                sib_copy(t).wait_recv()
                mine = 2 * t + core

                @pl.when(has)
                def _():
                    make(s).wait_recv()
                    total = wp[mine].astype(F32) + sib[t].astype(F32) + arrived[s].astype(F32)
                    wp[mine] = total.astype(BF16)

                @pl.when(jnp.logical_not(has))
                def _():
                    wp[mine] = (wp[mine].astype(F32) + sib[t].astype(F32)).astype(BF16)

                make(s).start()

            pending.append((s >= 0, functools.partial(make, s)))

    reduce_step(0)
    for e in range(2, nz - 1):
        gather_step(e)
        gather_use(e)
    for time in range(1, nz - 1):
        reduce_step(time)
        if time == 1:
            output(n_cp, att, w_all, out_ref, row_slice, shard, cols)

    def sum_ga(b, carry):
        at = row_slice(b)
        total = gar[0, at, :].astype(F32)
        for e in range(1, n_cp):
            total = total + gar[e, at, :].astype(F32)
        gsum[at, :] = total.astype(BF16)
        return carry

    dka[...] = jnp.zeros_like(dka)
    dva[...] = jnp.zeros_like(dva)

    def dq_copy(b):
        return remote(
            dqs.at[b], dqr.at[c], dq_s.at[b], dq_r.at[lax.rem(b - c + n_cp, n_cp)], d, b
        )

    def kv_copy(b):
        return remote(
            kvs.at[b], kvr.at[c], kv_s.at[b], kv_r.at[lax.rem(b - c + n_cp, n_cp)], d, b
        )

    def send_back(b, source, target, make):
        @pl.when(c == b)
        def _():
            target[c] = source[b]

        start(c != b, functools.partial(make, b))

    for b in reversed(range(n_cp)):
        last = (b + 1) * rows
        if b in (n_cp - 1, half_blocks - 1):
            h = b // half_blocks
            for j in range(1, n_cp):
                ga_copy(lax.rem(c + j, n_cp), h).wait_recv()
            lax.fori_loop(h * half_blocks, (h + 1) * half_blocks, sum_ga, 0)

        def body(r, carry, b=b, last=last):
            col = head_col(r)
            q = qh[b * rows : last, col]
            p = prob[r, b * rows : last, :last]
            g = gsum[b * rows : last, col]
            gp = dot_nt(g, vh[:last, :])
            delta = jnp.sum(p * gp, axis=1, keepdims=True)
            ds = (p * (gp - delta)).astype(BF16)
            dqs[b, :, col] = (dot_nn(ds, kh[:last, :]) * SCALE).astype(BF16)
            dka[:last, :] += dot_tn(ds, q)
            dva[:last, :] += dot_tn(p.astype(BF16), g)
            return carry

        lax.fori_loop(0, share, body, 0)
        send_back(b, dqs, dqr, dq_copy)
    for b in range(n_cp):
        at = slice(b * rows, (b + 1) * rows)
        kvs[b, :, :HD] = (dka[at, :] * SCALE).astype(BF16)
        kvs[b, :, HD:] = dva[at, :].astype(BF16)
        send_back(b, kvs, kvr, kv_copy)

    sib_copy(z).wait_recv()
    dw_ref[...] = wp[2 * z + core].astype(F32) + sib[z].astype(F32)

    @pl.when(has_left)
    def _():
        s = jnp.minimum(nz - 1 - z, nz - 2)
        remote(wp.at[d], fr.at[s], fr_s.at[s], fr_r.at[s], d + 2, c).wait_recv()
        dw_ref[...] += fr[s].astype(F32)

    @pl.when(has_right)
    def _():
        s = jnp.minimum(z, nz - 2)
        remote(wp.at[d], fl.at[s], fl_s.at[s], fl_r.at[s], d - 2, c).wait_recv()
        dw_ref[...] += fl[s].astype(F32)

    for j in range(1, n_cp):
        peer = lax.rem(c + j, n_cp)
        remote(dqs.at[peer], dqr.at[c], dq_s.at[peer], dq_r.at[j], d, peer).wait_recv()
        remote(kvs.at[peer], kvr.at[c], kv_s.at[peer], kv_r.at[j], d, peer).wait_recv()
    for e in range(n_cp):
        dq_ref[:, e * width : (e + 1) * width] = dqr[e]
    for h in range(HK):
        total = kvr[h * copies].astype(F32)
        for e in range(1, copies):
            total = total + kvr[h * copies + e].astype(F32)
        dk_ref[:, h * HD : (h + 1) * HD] = total[:, :HD].astype(BF16)
        dv_ref[:, h * HD : (h + 1) * HD] = total[:, HD:].astype(BF16)

    for cond, make in pending:
        if cond is None:
            make().wait_send()
        else:
            pl.when(cond)(functools.partial(lambda m: m().wait_send(), make))
    for t in range(n_cp):
        for h in range(2):
            pl.when(c != t)(functools.partial(lambda t, h: ga_copy(t, h).wait_send(), t, h))
        sib_copy(t).wait_send()


def output(n_cp, att, w_all, out_ref, row_slice, shard, cols):
    def body(b, carry):
        at = row_slice(b)
        total = jnp.zeros((out_ref.shape[0] // n_cp, cols), F32)
        for t in range(n_cp):
            unit = w_all[2 * t : 2 * t + 2].reshape(2 * shard, cols)
            total = total + dot_nn(att[t, at, :], unit)
        out_ref[at, :] = total.astype(BF16)
        return carry

    lax.fori_loop(0, n_cp, body, 0)


def per_device(n_dp, n_cp, queries, key_heads, value_heads, segment_ids, out_weight, grad_out):
    rows = queries.shape[0]
    group = rows * n_cp
    width = queries.shape[1] // n_cp
    shard, cols = out_weight.shape
    nz = n_dp // 2
    segments = jnp.broadcast_to(segment_ids, (8, rows))
    vmem = pl.BlockSpec(memory_space=pltpu.VMEM)
    dma = pltpu.SemaphoreType.DMA
    block = jax.ShapeDtypeStruct
    return pl.pallas_call(
        functools.partial(kernel, n_dp, n_cp),
        out_shape=(
            block((group, cols), BF16),
            block(queries.shape, BF16),
            block(key_heads.shape, BF16),
            block(value_heads.shape, BF16),
            block((shard, cols), F32),
        ),
        in_specs=[vmem] * 6,
        out_specs=[vmem] * 5,
        scratch_shapes=[
            pltpu.VMEM((group, width), BF16),
            pltpu.VMEM((group, HD), BF16),
            pltpu.VMEM((group, HD), BF16),
            pltpu.VMEM((n_cp, 8, rows), jnp.int32),
            pltpu.VMEM((group, group), F32),
            pltpu.VMEM((n_dp, shard, cols), BF16),
            pltpu.VMEM((n_cp, group, width), BF16),
            pltpu.VMEM((n_dp, shard, cols), BF16),
            pltpu.VMEM((nz, shard, cols), BF16),
            pltpu.VMEM((nz - 1, shard, cols), BF16),
            pltpu.VMEM((nz - 1, shard, cols), BF16),
            pltpu.VMEM((n_cp, group, width), BF16),
            pltpu.VMEM((n_cp, group, width), BF16),
            pltpu.VMEM((group, width), BF16),
            pltpu.VMEM((n_cp, rows, width), BF16),
            pltpu.VMEM((n_cp, rows, width), BF16),
            pltpu.VMEM((group, HD), F32),
            pltpu.VMEM((group, HD), F32),
            pltpu.VMEM((n_cp, rows, 2 * HD), BF16),
            pltpu.VMEM((n_cp, rows, 2 * HD), BF16),
            pltpu.VMEM((width // HD, group, group), F32),
            dma((4, n_cp)), dma((4, n_cp)),
            dma((nz - 1,)), dma((nz - 1,)), dma((nz - 1,)), dma((nz - 1,)),
            dma((2 * nz - 1,)), dma((2 * nz - 1,)),
            dma((2, n_cp)), dma((2, n_cp)),
            dma((2, n_cp)), dma((2, n_cp)),
            dma((nz,)), dma((nz,)),
            dma((nz - 1,)), dma((nz - 1,)), dma((nz - 1,)), dma((nz - 1,)),
            dma((n_cp,)), dma((n_cp,)), dma((n_cp,)), dma((n_cp,)),
        ],
        compiler_params=pltpu.CompilerParams(
            collective_id=0, has_side_effects=True, vmem_limit_bytes=60 * 1024 * 1024
        ),
    )(queries, key_heads, value_heads, segments, out_weight, grad_out)


def solution(mesh):
    rows = P(("dp", "cp"), None)
    grid = P("dp", "cp")
    return jax.shard_map(
        functools.partial(per_device, mesh.shape["dp"], mesh.shape["cp"]),
        mesh=mesh,
        in_specs=(rows, rows, rows, grid, grid, grid),
        out_specs=(grid, rows, rows, rows, grid),
        check_vma=False,
    )
```

```python
import functools
import math

import jax
import jax.numpy as jnp
from jax import lax
from jax.experimental import pallas as pl
from jax.experimental.pallas import tpu as pltpu
from jax.sharding import PartitionSpec as P

HQ = 24
HK = 4
HD = 128
SCALE = 1.0 / math.sqrt(HD)
MESH = pl.DeviceIdType.MESH
F32 = jnp.float32
BF16 = jnp.bfloat16


def dot_nt(a, b):
    return lax.dot_general(a, b, (((1,), (1,)), ((), ())), preferred_element_type=F32)


def dot_tn(a, b):
    return lax.dot_general(a, b, (((0,), (0,)), ((), ())), preferred_element_type=F32)


def dot_nn(a, b):
    return jnp.dot(a, b, preferred_element_type=F32)


def kernel(
    n_dp, n_cp,
    q_ref, k_ref, v_ref, seg_ref, w_ref, go_ref,
    out_ref, dq_ref, dk_ref, dv_ref, dw_ref,
    qh, kh, vh, sg, bias, w_all, att, wp, sib, fr, fl, gas, gar, gsum, dqs, dqr, dka, dva, kvs, kvr, prob,
    in_s, in_r, wr_s, wr_r, wl_s, wl_r, ws_s, ws_r, att_s, att_r, ga_s, ga_r,
    sb_s, sb_r, fr_s, fr_r, fl_s, fl_r, dq_s, dq_r, kv_s, kv_r,
):
    d = lax.axis_index("dp")
    c = lax.axis_index("cp")
    nz = n_dp // 2
    z = d // 2
    core = lax.rem(d, 2)
    sibling = d + 1 - 2 * core
    rows = q_ref.shape[0]
    group = rows * n_cp
    width = q_ref.shape[1] // n_cp
    share = width // HD
    copies = n_cp // HK
    shard, cols = w_ref.shape
    has_left = z > 0
    has_right = z < nz - 1
    pending = []

    def remote(src, dst, send, recv, dp, cp):
        return pltpu.make_async_remote_copy(
            src_ref=src, dst_ref=dst, send_sem=send, recv_sem=recv,
            device_id=(dp, cp), device_id_type=MESH,
        )

    def start(cond, make):
        pending.append((cond, make))
        if cond is None:
            make().start()
        else:
            pl.when(cond)(lambda: make().start())

    def wait_recv(cond, make):
        if cond is None:
            make().wait_recv()
        else:
            pl.when(cond)(lambda: make().wait_recv())

    barrier = pltpu.get_barrier_semaphore()

    def greet(dp, cp):
        pl.semaphore_signal(barrier, inc=1, device_id=(dp, cp), device_id_type=MESH)

    for j in range(1, n_cp):
        greet(d, lax.rem(c + j, n_cp))
    greet(sibling, c)
    pl.when(has_left)(lambda: greet(d - 2, c))
    pl.when(has_right)(lambda: greet(d + 2, c))
    pl.semaphore_wait(barrier, n_cp + jnp.where(has_left, 1, 0) + jnp.where(has_right, 1, 0))

    def w_right(s):
        slot = jnp.maximum(2 * (z - s) + core, 0)
        return remote(w_all.at[slot], w_all.at[slot], wr_s.at[s], wr_r.at[s], d + 2, c)

    def w_left(s):
        slot = jnp.minimum(2 * (z + s) + core, n_dp - 1)
        return remote(w_all.at[slot], w_all.at[slot], wl_s.at[s], wl_r.at[s], d - 2, c)

    def w_sib(slot, i):
        return remote(w_all.at[slot], w_all.at[slot], ws_s.at[i], ws_r.at[i], sibling, c)

    def row_slice(b):
        return pl.ds(pl.multiple_of(b * rows, rows), rows)

    def in_copies(j):
        peer = lax.rem(c + j, n_cp)
        qc = pl.ds(pl.multiple_of(peer * width, HD), width)
        kc = pl.ds(pl.multiple_of((peer // copies) * HD, HD), HD)
        mine = row_slice(c)
        pairs = (
            (q_ref.at[:, qc], qh.at[mine]),
            (k_ref.at[:, kc], kh.at[mine]),
            (v_ref.at[:, kc], vh.at[mine]),
            (seg_ref, sg.at[c]),
        )
        return [
            functools.partial(remote, a, b, in_s.at[i, j], in_r.at[i, j], d, peer)
            for i, (a, b) in enumerate(pairs)
        ]

    for j in range(1, n_cp):
        for make in in_copies(j):
            start(None, make)
    w_all[d] = w_ref[...]
    start(has_right, functools.partial(w_right, 0))
    start(has_left, functools.partial(w_left, 0))
    start(None, functools.partial(w_sib, d, 0))

    own_q = pl.ds(pl.multiple_of(c * width, HD), width)
    own_k = pl.ds(pl.multiple_of((c // copies) * HD, HD), HD)
    qh[row_slice(c), :] = q_ref[:, own_q]
    kh[row_slice(c), :] = k_ref[:, own_k]
    vh[row_slice(c), :] = v_ref[:, own_k]
    sg[c] = seg_ref[...]

    half = group // 2
    half_blocks = n_cp // 2

    def ga_copy(t, h):
        part = pl.ds(h * half, half)
        j = lax.rem(t - c + n_cp, n_cp)
        return remote(gas.at[t, part], gar.at[c, part], ga_s.at[h, t], ga_r.at[h, j], d, t)

    def ga_unit(t):
        def body(b, carry):
            unit = w_all[pl.ds(2 * t, 2)].reshape(2 * shard, cols)
            gas[t, row_slice(b), :] = dot_nt(go_ref[row_slice(b), :], unit).astype(BF16)
            return carry

        for h in (1, 0):
            lax.fori_loop(h * half_blocks, (h + 1) * half_blocks, body, 0)

            @pl.when(t != c)
            def _(h=h):
                ga_copy(t, h).start()

        @pl.when(t == c)
        def _():
            gar[c] = gas[t]

    def gather_step(s):
        left_on, right_on = z - 1 - s >= 0, z + 1 + s < nz
        wait_recv(left_on, functools.partial(w_right, s))
        wait_recv(right_on, functools.partial(w_left, s))
        if s + 1 < nz - 1:
            start(left_on & has_right, functools.partial(w_right, s + 1))
            start(right_on & has_left, functools.partial(w_left, s + 1))
        lslot = jnp.maximum(2 * (z - 1 - s) + core, 0)
        rslot = jnp.minimum(2 * (z + 1 + s) + core, n_dp - 1)
        start(left_on, functools.partial(w_sib, lslot, 1 + s))
        start(right_on, functools.partial(w_sib, rslot, nz + s))

    def gather_use(s):
        for on, i, t in ((z - 1 - s >= 0, 1 + s, z - 1 - s), (z + 1 + s < nz, nz + s, z + 1 + s)):

            @pl.when(on)
            def _(i=i, t=t):
                w_sib(d, i).wait_recv()
                ga_unit(t)

    w_sib(d, 0).wait_recv()
    ga_unit(z)
    gather_step(0)
    for j in range(1, n_cp):
        for make in in_copies(j):
            wait_recv(None, make)

    ones = jnp.ones((8, HD), BF16)
    for b in range(n_cp):
        at = slice(b * rows, (b + 1) * rows)
        seg_col = dot_tn(sg[b].astype(F32).astype(BF16), ones)[:, :1] * 0.125
        seg_row = jnp.concatenate([sg[e][:1, :] for e in range(n_cp)], axis=1).astype(F32)
        i = lax.broadcasted_iota(jnp.int32, (rows, group), 0) + b * rows
        jj = lax.broadcasted_iota(jnp.int32, (rows, group), 1)
        bias[at, :] = jnp.where((jj <= i) & (seg_col == seg_row), 0.0, -1e30)

    def probability(b, col):
        last = (b + 1) * rows
        q = qh[b * rows : last, col]
        s = dot_nt(q, kh[:last, :]) * SCALE + bias[b * rows : last, :last]
        e = jnp.exp(s - jnp.max(s, axis=1, keepdims=True))
        return e / jnp.sum(e, axis=1, keepdims=True)

    def head_col(r):
        return pl.ds(pl.multiple_of(r * HD, HD), HD)

    def forward(b):
        def body(r, carry):
            col = head_col(r)
            p = probability(b, col)
            prob[r, b * rows : (b + 1) * rows, : (b + 1) * rows] = p
            a = dot_nn(p.astype(BF16), vh[: (b + 1) * rows, :]).astype(BF16)
            att[c, b * rows : (b + 1) * rows, col] = a
            return carry

        lax.fori_loop(0, share, body, 0)

    def att_copy(j, h):
        part = att.at[c, pl.ds(h * half, half)]
        return remote(part, part, att_s.at[h, j], att_r.at[h, j], d, lax.rem(c + j, n_cp))

    for h in range(2):
        for b in range(h * n_cp // 2, (h + 1) * n_cp // 2):
            forward(b)
        for j in range(1, n_cp):
            start(None, functools.partial(att_copy, j, h))
    for e in range(1, nz - 1):
        gather_step(e)
        gather_use(e - 1)
    gather_use(nz - 2)

    def sib_copy(t):
        return remote(
            wp.at[2 * t + 1 - core], sib.at[t], sb_s.at[t], sb_r.at[t], sibling, c
        )

    def weight_unit(j, carry):
        t = lax.rem(c - j + n_cp, n_cp)

        @pl.when(j > 0)
        def _():
            att_copy(j, 0).wait_recv()
            att_copy(j, 1).wait_recv()

        part = dot_tn(att[t], go_ref[...]).astype(BF16)
        wp[pl.ds(2 * t, 2)] = part.reshape(2, shard, cols)
        sib_copy(t).start()
        return carry

    lax.fori_loop(0, n_cp, weight_unit, 0)

    def right_copy(s):
        t = nz - 1 - s
        return remote(wp.at[2 * t + core], fr.at[s], fr_s.at[s], fr_r.at[s], d + 2, c)

    def left_copy(s):
        return remote(wp.at[2 * s + core], fl.at[s], fl_s.at[s], fl_r.at[s], d - 2, c)

    def reduce_step(time):
        right, left = time - z, time - (nz - 1 - z)
        for s, t, has, make, arrived in (
            (right, nz - 1 - right, has_left, right_copy, fr),
            (left, left, has_right, left_copy, fl),
        ):

            @pl.when(s >= 0)
            def _(s=s, t=t, has=has, make=make, arrived=arrived):
                sib_copy(t).wait_recv()
                mine = 2 * t + core

                @pl.when(has)
                def _():
                    make(s).wait_recv()
                    total = wp[mine].astype(F32) + sib[t].astype(F32) + arrived[s].astype(F32)
                    wp[mine] = total.astype(BF16)

                @pl.when(jnp.logical_not(has))
                def _():
                    wp[mine] = (wp[mine].astype(F32) + sib[t].astype(F32)).astype(BF16)

                make(s).start()

            pending.append((s >= 0, functools.partial(make, s)))

    reduce_step(0)
    for time in range(1, nz - 1):
        reduce_step(time)
        if time == 1:
            output(n_cp, att, w_all, out_ref, row_slice, shard, cols)

    def sum_ga(b, carry):
        at = row_slice(b)
        total = gar[0, at, :].astype(F32)
        for e in range(1, n_cp):
            total = total + gar[e, at, :].astype(F32)
        gsum[at, :] = total.astype(BF16)
        return carry

    dka[...] = jnp.zeros_like(dka)
    dva[...] = jnp.zeros_like(dva)

    def dq_copy(b):
        return remote(
            dqs.at[b], dqr.at[c], dq_s.at[b], dq_r.at[lax.rem(b - c + n_cp, n_cp)], d, b
        )

    def kv_copy(b):
        return remote(
            kvs.at[b], kvr.at[c], kv_s.at[b], kv_r.at[lax.rem(b - c + n_cp, n_cp)], d, b
        )

    def send_back(b, source, target, make):
        @pl.when(c == b)
        def _():
            target[c] = source[b]

        start(c != b, functools.partial(make, b))

    for b in reversed(range(n_cp)):
        last = (b + 1) * rows
        if b in (n_cp - 1, half_blocks - 1):
            h = b // half_blocks
            for j in range(1, n_cp):
                ga_copy(lax.rem(c + j, n_cp), h).wait_recv()
            lax.fori_loop(h * half_blocks, (h + 1) * half_blocks, sum_ga, 0)

        def body(r, carry, b=b, last=last):
            col = head_col(r)
            q = qh[b * rows : last, col]
            p = prob[r, b * rows : last, :last]
            g = gsum[b * rows : last, col]
            gp = dot_nt(g, vh[:last, :])
            delta = jnp.sum(p * gp, axis=1, keepdims=True)
            ds = (p * (gp - delta)).astype(BF16)
            dqs[b, :, col] = (dot_nn(ds, kh[:last, :]) * SCALE).astype(BF16)
            dka[:last, :] += dot_tn(ds, q)
            dva[:last, :] += dot_tn(p.astype(BF16), g)
            return carry

        lax.fori_loop(0, share, body, 0)
        send_back(b, dqs, dqr, dq_copy)
    for b in range(n_cp):
        at = slice(b * rows, (b + 1) * rows)
        kvs[b, :, :HD] = (dka[at, :] * SCALE).astype(BF16)
        kvs[b, :, HD:] = dva[at, :].astype(BF16)
        send_back(b, kvs, kvr, kv_copy)

    sib_copy(z).wait_recv()
    dw_ref[...] = wp[2 * z + core].astype(F32) + sib[z].astype(F32)

    @pl.when(has_left)
    def _():
        s = jnp.minimum(nz - 1 - z, nz - 2)
        remote(wp.at[d], fr.at[s], fr_s.at[s], fr_r.at[s], d + 2, c).wait_recv()
        dw_ref[...] += fr[s].astype(F32)

    @pl.when(has_right)
    def _():
        s = jnp.minimum(z, nz - 2)
        remote(wp.at[d], fl.at[s], fl_s.at[s], fl_r.at[s], d - 2, c).wait_recv()
        dw_ref[...] += fl[s].astype(F32)

    for j in range(1, n_cp):
        peer = lax.rem(c + j, n_cp)
        remote(dqs.at[peer], dqr.at[c], dq_s.at[peer], dq_r.at[j], d, peer).wait_recv()
        remote(kvs.at[peer], kvr.at[c], kv_s.at[peer], kv_r.at[j], d, peer).wait_recv()
    for e in range(n_cp):
        dq_ref[:, e * width : (e + 1) * width] = dqr[e]
    for h in range(HK):
        total = kvr[h * copies].astype(F32)
        for e in range(1, copies):
            total = total + kvr[h * copies + e].astype(F32)
        dk_ref[:, h * HD : (h + 1) * HD] = total[:, :HD].astype(BF16)
        dv_ref[:, h * HD : (h + 1) * HD] = total[:, HD:].astype(BF16)

    for cond, make in pending:
        if cond is None:
            make().wait_send()
        else:
            pl.when(cond)(functools.partial(lambda m: m().wait_send(), make))
    for t in range(n_cp):
        for h in range(2):
            pl.when(c != t)(functools.partial(lambda t, h: ga_copy(t, h).wait_send(), t, h))
        sib_copy(t).wait_send()


def output(n_cp, att, w_all, out_ref, row_slice, shard, cols):
    def body(b, carry):
        at = row_slice(b)
        total = jnp.zeros((out_ref.shape[0] // n_cp, cols), F32)
        for t in range(n_cp):
            unit = w_all[2 * t : 2 * t + 2].reshape(2 * shard, cols)
            total = total + dot_nn(att[t, at, :], unit)
        out_ref[at, :] = total.astype(BF16)
        return carry

    lax.fori_loop(0, n_cp, body, 0)


def per_device(n_dp, n_cp, queries, key_heads, value_heads, segment_ids, out_weight, grad_out):
    rows = queries.shape[0]
    group = rows * n_cp
    width = queries.shape[1] // n_cp
    shard, cols = out_weight.shape
    nz = n_dp // 2
    segments = jnp.broadcast_to(segment_ids, (8, rows))
    vmem = pl.BlockSpec(memory_space=pltpu.VMEM)
    dma = pltpu.SemaphoreType.DMA
    block = jax.ShapeDtypeStruct
    return pl.pallas_call(
        functools.partial(kernel, n_dp, n_cp),
        out_shape=(
            block((group, cols), BF16),
            block(queries.shape, BF16),
            block(key_heads.shape, BF16),
            block(value_heads.shape, BF16),
            block((shard, cols), F32),
        ),
        in_specs=[vmem] * 6,
        out_specs=[vmem] * 5,
        scratch_shapes=[
            pltpu.VMEM((group, width), BF16),
            pltpu.VMEM((group, HD), BF16),
            pltpu.VMEM((group, HD), BF16),
            pltpu.VMEM((n_cp, 8, rows), jnp.int32),
            pltpu.VMEM((group, group), F32),
            pltpu.VMEM((n_dp, shard, cols), BF16),
            pltpu.VMEM((n_cp, group, width), BF16),
            pltpu.VMEM((n_dp, shard, cols), BF16),
            pltpu.VMEM((nz, shard, cols), BF16),
            pltpu.VMEM((nz - 1, shard, cols), BF16),
            pltpu.VMEM((nz - 1, shard, cols), BF16),
            pltpu.VMEM((n_cp, group, width), BF16),
            pltpu.VMEM((n_cp, group, width), BF16),
            pltpu.VMEM((group, width), BF16),
            pltpu.VMEM((n_cp, rows, width), BF16),
            pltpu.VMEM((n_cp, rows, width), BF16),
            pltpu.VMEM((group, HD), F32),
            pltpu.VMEM((group, HD), F32),
            pltpu.VMEM((n_cp, rows, 2 * HD), BF16),
            pltpu.VMEM((n_cp, rows, 2 * HD), BF16),
            pltpu.VMEM((width // HD, group, group), F32),
            dma((4, n_cp)), dma((4, n_cp)),
            dma((nz - 1,)), dma((nz - 1,)), dma((nz - 1,)), dma((nz - 1,)),
            dma((2 * nz - 1,)), dma((2 * nz - 1,)),
            dma((2, n_cp)), dma((2, n_cp)),
            dma((2, n_cp)), dma((2, n_cp)),
            dma((nz,)), dma((nz,)),
            dma((nz - 1,)), dma((nz - 1,)), dma((nz - 1,)), dma((nz - 1,)),
            dma((n_cp,)), dma((n_cp,)), dma((n_cp,)), dma((n_cp,)),
        ],
        compiler_params=pltpu.CompilerParams(
            collective_id=0, has_side_effects=True, vmem_limit_bytes=60 * 1024 * 1024
        ),
    )(queries, key_heads, value_heads, segments, out_weight, grad_out)


def solution(mesh):
    rows = P(("dp", "cp"), None)
    grid = P("dp", "cp")
    return jax.shard_map(
        functools.partial(per_device, mesh.shape["dp"], mesh.shape["cp"]),
        mesh=mesh,
        in_specs=(rows, rows, rows, grid, grid, grid),
        out_specs=(grid, rows, rows, rows, grid),
        check_vma=False,
    )
```
